128 devices in a mesh: ctx: 16 (over x, y), ch: 8 (over z, core).
Axes of the slice: x: 4, y: 4, z: 4, core: 2. Of those that a mesh axis runs over, the one named last changes fastest.
Arguments:
- keyed_values: bfloat16 [2048, 8192], P('ctx', 'ch'), may hold values from -6 to 6
- gate_values: bfloat16 [2048, 8192], P('ctx', 'ch'), may hold values from -6 to 6
- long_filter: float32 [2048, 8192], P('ctx', 'ch'), may hold values from -0.125 to 0.125
- skip_bias: float32 [8192], P('ch'), may hold values from -1 to 1
- out_weight: bfloat16 [8192, 8192], P('ch'), may hold values from -0.09375 to 0.09375
Outputs:
- mixed: float32 [2048, 8192], P('ctx', 'ch')
The draws below stay inside these ranges and needn't reach their ends.
All inputs are finite; a program needn't handle non-finite values.
Results may differ from the reference program's by a relative error of at most 0.023.
Values may be sent and summed in bfloat16 or wider, within the bound.
A program may use at most 128 MiB of HBM per device.

```python
import jax
import jax.numpy as jnp
from jax import lax

D = 8192
TOKENS = 2048
CH_DEV = 1024


def strengthened(entries, rng, source, target, parts, factor):
    owner, partner = [(jnp.arange(entries.shape[dim]) // (entries.shape[dim] // parts)).reshape([-1 if axis == dim else 1 for axis in range(entries.ndim)]) for dim in (source, target)]
    chosen = jax.random.permutation(rng, parts)[partner]
    strong = (owner == chosen) | (owner == (partner + parts // 2) % parts)
    return jnp.where(strong, factor * entries, entries)


def levels(rng, shape, split, low, largest):
    factor_of = 1.0
    for dim, parts in split:
        draws = jax.random.uniform(jax.random.fold_in(jax.random.fold_in(rng, 6), dim), (parts,), jnp.float32, low / len(split), largest / len(split))
        factor_of = factor_of * jnp.repeat(jnp.exp(draws), shape[dim] // parts).reshape((-1,) + (1,) * (len(shape) - 1 - dim))
    return factor_of


def bell_draw(own_key, extent, spread, limit, split=(), held_as=jnp.bfloat16):
    array = jax.random.normal(own_key, extent, jnp.float32) * spread
    if len(split) > 0:
        array = levels(own_key, extent, split, -0.22, 0.18) * array
    return jnp.clip(array, min=-limit, max=limit).astype(held_as)


def bell_draw_with(stream_key, dims, scale, reach, shards, heavy, held_as=jnp.bfloat16):
    result = scale * jax.random.normal(stream_key, dims, jnp.float32)
    if shards:
        result = result * levels(stream_key, dims, shards, -0.22, 0.18)
    return jnp.clip(strengthened(result, jax.random.fold_in(stream_key, 3), *heavy), -reach, reach).astype(held_as)


def setup_inputs(seed: int = 0) -> dict:
    seeds = jax.random.split(jax.random.key(seed), 6)
    keyed_values = bell_draw(seeds[0], (TOKENS, D), 1.0, 6.0, ((0, 16), (1, 8)))
    gate_values = bell_draw(seeds[1], (TOKENS, D), 1.0, 6.0, ((0, 16), (1, 8)))
    long_filter = bell_draw(seeds[2], (TOKENS, D), TOKENS ** -0.5, 0.125, ((0, 16), (1, 8)), jnp.float32)
    skip_bias = jnp.clip(jax.random.uniform(seeds[3], (D,), jnp.float32, -1.0, 1.0) * levels(seeds[3], (D,), ((0, 8),), -0.4, 0.0), -1.0, 1.0)
    out_weight = bell_draw_with(seeds[4], (D, D), D ** -0.5, 0.09375, ((0, 8),), (0, 1, 8, 2.0))
    return {"keyed_values": keyed_values, "gate_values": gate_values, "long_filter": long_filter, "skip_bias": skip_bias, "out_weight": out_weight}


def causal_conv(values, filters):
    full_length = 2 * values.shape[0]
    spectrum = jnp.fft.rfft(values, n=full_length, axis=0) * jnp.fft.rfft(filters, n=full_length, axis=0)
    return jnp.fft.irfft(spectrum, n=full_length, axis=0)[: values.shape[0]]


def reference(keyed_values, gate_values, long_filter, skip_bias, out_weight):
    values32 = keyed_values.astype(jnp.float32)
    convolved = causal_conv(values32, long_filter)
    gated_rows = ((convolved + skip_bias * values32) * gate_values.astype(jnp.float32)).astype(jnp.bfloat16)
    block_inputs = gated_rows.reshape(TOKENS, D // CH_DEV, CH_DEV).transpose(1, 0, 2)
    block_weights = out_weight.reshape(D // CH_DEV, CH_DEV, D)

    def accumulate(carried, pair):
        partial_value = jnp.dot(pair[0].astype(jnp.float32), pair[1].astype(jnp.float32), preferred_element_type=jnp.float32)
        rounded = lax.optimization_barrier(partial_value.astype(jnp.bfloat16))
        return carried + rounded.astype(jnp.float32), None

    total, unused = lax.scan(accumulate, jnp.zeros((TOKENS, D), jnp.float32), (block_inputs, block_weights))
    return total
```

```python
import functools
import math

import jax
import jax.numpy as jnp
import ml_dtypes
import numpy as np
from jax import lax
from jax.experimental import pallas as pl
from jax.experimental.pallas import tpu as pltpu
from jax.sharding import PartitionSpec as P

MESH = pl.DeviceIdType.MESH
SIDE = 4
BLOCKS = 16
ROWS = 128
LANES = 128
HALF = 64
FULL = 2 * BLOCKS * ROWS
GROUP = 16
ROUTES = ((2, 2), (2, 1), (1, 2), (2, 3), (3, 2), (2, 0), (0, 2), (1, 1), (3, 3), (1, 3), (3, 1),
          (1, 0), (3, 0), (0, 1), (0, 3))


@functools.cache
def tables():
    a = np.arange(BLOCKS)
    forward = np.zeros((16, 2, BLOCKS))
    inverse = np.zeros((BLOCKS, 16, 2))
    for k1 in range(16):
        angle = 2 * math.pi * a * k1 / 32
        forward[k1, 0] = np.cos(angle)
        forward[k1, 1] = -np.sin(angle)
        inverse[:, k1, 0] = 2 * np.cos(angle)
        inverse[:, k1, 1] = -2 * np.sin(angle)
    forward[0, 1] = (-1.0) ** a
    inverse[:, 0, 0] = 1.0
    inverse[:, 0, 1] = (-1.0) ** a
    eye = np.eye(GROUP)
    first = np.kron(forward.reshape(32, BLOCKS), eye)
    last = np.kron(inverse.reshape(BLOCKS, 32) / 32, eye)
    b = np.arange(ROWS)
    middle = np.zeros((16, 256, 256))
    middle_back = np.zeros((16, 256, 256))
    for k1 in range(1, 16):
        angle = 2 * math.pi * np.outer(k1 + 32 * b, b) / FULL
        c, s = np.cos(angle), np.sin(angle)
        middle[k1] = np.block([[c, s], [-s, c]])
        middle_back[k1] = np.block([[c.T, -s.T], [s.T, c.T]]) / 128
    k2 = np.arange(64)
    angle = 2 * math.pi * np.outer(k2, b) / 128
    c, s = np.cos(angle), np.sin(angle)
    imag = -s
    imag[0] = (-1.0) ** b
    middle[0, 0:64, 0:128] = c
    middle[0, 128:192, 0:128] = imag
    weight = np.full((64, 1), 2.0)
    weight[0] = 1.0
    middle_back[0, 0:128, 0:64] = (weight * c).T / 128
    middle_back[0, 0:128, 128:192] = (weight * imag).T / 128
    angle = 2 * math.pi * np.outer(16 + 32 * k2, b) / FULL
    c, s = np.cos(angle), np.sin(angle)
    middle[0, 64:128, 128:256] = c
    middle[0, 192:256, 128:256] = -s
    middle_back[0, 128:256, 64:128] = 2 * c.T / 128
    middle_back[0, 128:256, 192:256] = -2 * s.T / 128
    return tuple(t.astype(ml_dtypes.bfloat16) for t in (first, middle, middle_back, last))


def dot(left, right):
    return jnp.dot(left, right, preferred_element_type=jnp.float32)


def kernel(v_hbm, g_hbm, h_hbm, bias_ref, w_hbm, f1_hbm, m_hbm, mb_hbm, f2_hbm, out_ref,
           v, g, h, w, f1, m, mb, f2, send, recv, mid, back, bsend, brecv, gated, psend, precv, ring_s, ring_r,
           keep, in_sem, w_sem, s_sem, r_sem, bs_sem, br_sem, ps_sem, pr_sem, rs_sem, rr_sem):
    ctx, ch = lax.axis_index("ctx"), lax.axis_index("ch")
    x, y = ctx // SIDE, lax.rem(ctx, SIDE)
    z, core = ch // 2, lax.rem(ch, 2)

    def shifted(position, by):
        return lax.rem(position + by, SIDE)

    partners = [shifted(x, dx) * SIDE + shifted(y, dy) for dx, dy in ROUTES]
    other = (ctx, z * 2 + 1 - core)
    up = (ctx, shifted(z, 1) * 2 + core)
    down = (ctx, shifted(z, 3) * 2 + core)

    barrier = pltpu.get_barrier_semaphore()
    for partner in partners:
        pl.semaphore_signal(barrier, inc=1, device_id=(partner, ch), device_id_type=MESH)
    for device in (other, up, down):
        pl.semaphore_signal(barrier, inc=1, device_id=device, device_id_type=MESH)

    loads = []
    for i, (src, dst) in enumerate(((h_hbm, h), (v_hbm, v), (f1_hbm, f1), (m_hbm, m), (mb_hbm, mb), (f2_hbm, f2), (g_hbm, g))):
        load = pltpu.make_async_copy(src, dst, in_sem.at[i])
        load.start()
        loads.append(load)
    w_load = pltpu.make_async_copy(w_hbm, w, w_sem)
    w_load.start()

    low = lax.broadcasted_iota(jnp.int32, (ROWS, LANES), 1) < HALF
    loads[0].wait()
    loads[1].wait()
    for t in range(8):
        columns = slice(t * LANES, (t + 1) * LANES)
        values, taps = v[:, columns].astype(jnp.float32), h[:, columns]
        send[2 * t] = jnp.where(low, values, pltpu.roll(taps, HALF, 1)).astype(jnp.bfloat16)
        send[2 * t + 1] = jnp.where(low, pltpu.roll(values, HALF, 1), taps).astype(jnp.bfloat16)

    pl.semaphore_wait(barrier, len(ROUTES) + 3)
    copies = []
    for i, partner in enumerate(partners):
        copy = pltpu.make_async_remote_copy(
            send.at[partner], recv.at[ctx], s_sem.at[i], r_sem.at[i], device_id=(partner, ch), device_id_type=MESH)
        copy.start()
        copies.append(copy)
    recv[ctx] = send[ctx]
    for i in range(2, 6):
        loads[i].wait()
    for copy in copies:
        copy.wait()

    for k in range(ROWS // GROUP):
        rows = slice(k * GROUP, (k + 1) * GROUP)
        part = dot(f1[...], recv[:, rows, :].reshape(BLOCKS * GROUP, LANES))
        mid[:, :, rows, :] = part.astype(jnp.bfloat16).reshape(16, 2, GROUP, LANES)
    low_half = lax.broadcasted_iota(jnp.int32, (HALF, LANES), 1) < HALF
    for s in range(16):
        spectrum = dot(m[s], mid[s].reshape(2 * ROWS, LANES))
        real, imag = spectrum[:ROWS], spectrum[ROWS:]
        real2, imag2 = pltpu.roll(real, HALF, 1), pltpu.roll(imag, HALF, 1)
        rr, ii = real * real2, imag * imag2
        prod_real, prod_imag = rr - ii, real * imag2 + imag * real2
        if s == 0:
            top = lax.broadcasted_iota(jnp.int32, (ROWS, LANES), 0) == 0
            prod_real, prod_imag = jnp.where(top, rr, prod_real), jnp.where(top, ii, prod_imag)
        product = jnp.concatenate([prod_real, prod_imag], axis=0).astype(jnp.bfloat16)
        turned = dot(mb[s], product)
        for part in range(2):
            first, second = turned[part * ROWS:part * ROWS + HALF], turned[part * ROWS + HALF:(part + 1) * ROWS]
            back[s, part] = jnp.where(low_half, first, second).astype(jnp.bfloat16)
    for k in range(HALF // GROUP):
        rows = slice(k * GROUP, (k + 1) * GROUP)
        part = dot(f2[...], back[:, :, rows, :].reshape(2 * 16 * GROUP, LANES))
        bsend[:, rows, :] = part.astype(jnp.bfloat16).reshape(BLOCKS, GROUP, LANES)

    copies = []
    for i, partner in enumerate(partners):
        copy = pltpu.make_async_remote_copy(
            bsend.at[partner], brecv.at[ctx], bs_sem.at[i], br_sem.at[i], device_id=(partner, ch), device_id_type=MESH)
        copy.start()
        copies.append(copy)
    brecv[ctx] = bsend[ctx]
    loads[6].wait()
    for copy in copies:
        copy.wait()

    for t in range(8):
        columns = slice(t * LANES, (t + 1) * LANES)
        even, odd = brecv[2 * t].astype(jnp.float32), brecv[2 * t + 1].astype(jnp.float32)
        for part in range(2):
            rows = slice(part * HALF, (part + 1) * HALF)
            if part == 0:
                convolved = jnp.where(low_half, even, pltpu.roll(odd, HALF, 1))
            else:
                convolved = jnp.where(low_half, pltpu.roll(even, HALF, 1), odd)
            values = v[rows, columns].astype(jnp.float32)
            gate = g[rows, columns].astype(jnp.float32)
            gated[rows, columns] = ((convolved + bias_ref[0:1, columns] * values) * gate).astype(jnp.bfloat16)

    w_load.wait()

    def project(distance, part, to_core):
        start = (shifted(z, distance) * 2 + to_core) * 1024 + part * 512
        return dot(gated[...], w[:, pl.ds(pl.multiple_of(start, 512), 512)])

    def to_other(distance, part):
        i = 2 * distance + part
        psend[i] = project(distance, part, 1 - core).astype(jnp.bfloat16)
        copy = pltpu.make_async_remote_copy(
            psend.at[i], precv.at[i], ps_sem.at[i], pr_sem.at[i], device_id=other, device_id_type=MESH)
        copy.start()
        return copy

    def ring(i, device):
        copy = pltpu.make_async_remote_copy(
            ring_s.at[i], ring_r.at[i], rs_sem.at[i], rr_sem.at[i], device_id=device, device_id_type=MESH)
        copy.start()
        return copy

    pair = {}
    rings = {}

    def pair_sum(distance, part):
        own = project(distance, part, core)
        pair[distance, part].wait_recv()
        return own + precv[2 * distance + part].astype(jnp.float32)

    for part in range(2):
        pair[2, part] = to_other(2, part)
    for part, device in ((0, up), (1, down)):
        ring_s[part] = pair_sum(2, part).astype(jnp.bfloat16)
        rings[part] = ring(part, device)
    pair[1, 1], pair[3, 0] = to_other(1, 1), to_other(3, 0)
    ring_s[2] = pair_sum(1, 1).astype(jnp.bfloat16)
    rings[2] = ring(2, up)
    ring_s[3] = pair_sum(3, 0).astype(jnp.bfloat16)
    rings[3] = ring(3, down)
    pair[1, 0], pair[3, 1] = to_other(1, 0), to_other(3, 1)
    for i, (distance, part, device) in ((4, (1, 0, up)), (5, (3, 1, down))):
        total = pair_sum(distance, part)
        rings[i - 4].wait_recv()
        ring_s[i] = (total + ring_r[i - 4].astype(jnp.float32)).astype(jnp.bfloat16)
        rings[i] = ring(i, device)
    for part in range(2):
        pair[0, part] = to_other(0, part)
    for part in range(2):
        keep[part] = pair_sum(0, part)
    for i in (2, 3):
        rings[i].wait_recv()
    rings[4].wait_recv()
    out_ref[:, 0:512] = keep[0] + (ring_r[4].astype(jnp.float32) + ring_r[3].astype(jnp.float32))
    rings[5].wait_recv()
    out_ref[:, 512:1024] = keep[1] + (ring_r[2].astype(jnp.float32) + ring_r[5].astype(jnp.float32))
    for copy in (*pair.values(), *rings.values()):
        copy.wait_send()


def on_device(keyed_values, gate_values, long_filter, skip_bias, out_weight):
    first, middle, middle_back, last = (jnp.asarray(t) for t in tables())
    bf, f32 = jnp.bfloat16, jnp.float32
    hbm = pl.BlockSpec(memory_space=pl.ANY)
    vmem = pl.BlockSpec(memory_space=pltpu.VMEM)
    dma = pltpu.SemaphoreType.DMA
    hops = len(ROUTES)
    return pl.pallas_call(
        kernel,
        out_shape=jax.ShapeDtypeStruct((ROWS, 1024), f32),
        in_specs=[hbm, hbm, hbm, vmem, hbm, hbm, hbm, hbm, hbm],
        out_specs=vmem,
        scratch_shapes=[
            pltpu.VMEM((ROWS, 1024), bf),
            pltpu.VMEM((ROWS, 1024), bf),
            pltpu.VMEM((ROWS, 1024), f32),
            pltpu.VMEM((1024, 8192), bf),
            pltpu.VMEM((512, 256), bf),
            pltpu.VMEM((16, 256, 256), bf),
            pltpu.VMEM((16, 256, 256), bf),
            pltpu.VMEM((256, 512), bf),
            pltpu.VMEM((BLOCKS, ROWS, LANES), bf),
            pltpu.VMEM((BLOCKS, ROWS, LANES), bf),
            pltpu.VMEM((16, 2, ROWS, LANES), bf),
            pltpu.VMEM((16, 2, HALF, LANES), bf),
            pltpu.VMEM((BLOCKS, HALF, LANES), bf),
            pltpu.VMEM((BLOCKS, HALF, LANES), bf),
            pltpu.VMEM((ROWS, 1024), bf),
            pltpu.VMEM((8, ROWS, 512), bf),
            pltpu.VMEM((8, ROWS, 512), bf),
            pltpu.VMEM((6, ROWS, 512), bf),
            pltpu.VMEM((6, ROWS, 512), bf),
            pltpu.VMEM((2, ROWS, 512), f32),
            dma((7,)),
            dma,
            dma((hops,)),
            dma((hops,)),
            dma((hops,)),
            dma((hops,)),
            dma((8,)),
            dma((8,)),
            dma((6,)),
            dma((6,)),
        ],
        compiler_params=pltpu.CompilerParams(
            collective_id=0, has_side_effects=True, vmem_limit_bytes=48 << 20),
        cost_estimate=pl.CostEstimate(flops=3 << 30, bytes_accessed=24 << 20, transcendentals=0),
    )(keyed_values, gate_values, long_filter, skip_bias.reshape(1, 1024), out_weight, first, middle, middle_back, last)


def solution(mesh):
    return jax.shard_map(
        on_device,
        mesh=mesh,
        in_specs=(P("ctx", "ch"), P("ctx", "ch"), P("ctx", "ch"), P("ch"), P("ch", None)),
        out_specs=P("ctx", "ch"),
        check_vma=False,
    )
```

```python
import functools
import math

import jax
import jax.numpy as jnp
import ml_dtypes
import numpy as np
from jax import lax
from jax.experimental import pallas as pl
from jax.experimental.pallas import tpu as pltpu
from jax.sharding import PartitionSpec as P

MESH = pl.DeviceIdType.MESH
SIDE = 4
BLOCKS = 16
ROWS = 128
LANES = 128
HALF = 64
FULL = 2 * BLOCKS * ROWS
GROUP = 16
ROUTES = ((2, 2), (2, 1), (1, 2), (2, 3), (3, 2), (2, 0), (0, 2), (1, 1), (3, 3), (1, 3), (3, 1),
          (1, 0), (3, 0), (0, 1), (0, 3))


@functools.cache
def tables():
    a = np.arange(BLOCKS)
    forward = np.zeros((16, 2, BLOCKS))
    inverse = np.zeros((BLOCKS, 16, 2))
    for k1 in range(16):
        angle = 2 * math.pi * a * k1 / 32
        forward[k1, 0] = np.cos(angle)
        forward[k1, 1] = -np.sin(angle)
        inverse[:, k1, 0] = 2 * np.cos(angle)
        inverse[:, k1, 1] = -2 * np.sin(angle)
    forward[0, 1] = (-1.0) ** a
    inverse[:, 0, 0] = 1.0
    inverse[:, 0, 1] = (-1.0) ** a
    eye = np.eye(GROUP)
    first = np.kron(forward.reshape(32, BLOCKS), eye)
    last = np.kron(inverse.reshape(BLOCKS, 32) / 32, eye)
    b = np.arange(ROWS)
    middle = np.zeros((16, 256, 256))
    middle_back = np.zeros((16, 256, 256))
    for k1 in range(1, 16):
        angle = 2 * math.pi * np.outer(k1 + 32 * b, b) / FULL
        c, s = np.cos(angle), np.sin(angle)
        middle[k1] = np.block([[c, s], [-s, c]])
        middle_back[k1] = np.block([[c.T, -s.T], [s.T, c.T]]) / 128
    k2 = np.arange(64)
    angle = 2 * math.pi * np.outer(k2, b) / 128
    c, s = np.cos(angle), np.sin(angle)
    imag = -s
    imag[0] = (-1.0) ** b
    middle[0, 0:64, 0:128] = c
    middle[0, 128:192, 0:128] = imag
    weight = np.full((64, 1), 2.0)
    weight[0] = 1.0
    middle_back[0, 0:128, 0:64] = (weight * c).T / 128
    middle_back[0, 0:128, 128:192] = (weight * imag).T / 128
    angle = 2 * math.pi * np.outer(16 + 32 * k2, b) / FULL
    c, s = np.cos(angle), np.sin(angle)
    middle[0, 64:128, 128:256] = c
    middle[0, 192:256, 128:256] = -s
    middle_back[0, 128:256, 64:128] = 2 * c.T / 128
    middle_back[0, 128:256, 192:256] = -2 * s.T / 128
    return tuple(t.astype(ml_dtypes.bfloat16) for t in (first, middle, middle_back, last))


def dot(left, right):
    return jnp.dot(left, right, preferred_element_type=jnp.float32)


def kernel(v_hbm, g_hbm, h_hbm, bias_hbm, w_hbm, f1_hbm, m_hbm, mb_hbm, f2_hbm, out_ref,
           v, g, h, bias_ref, w, f1, m, mb, f2, send, recv, mid, back, bsend, brecv, gated, psend, precv, ring_s, ring_r,
           keep, relay, in_sem, w_sem, s_sem, r_sem, bs_sem, br_sem, ps_sem, pr_sem, rs_sem, rr_sem):
    ctx, ch = lax.axis_index("ctx"), lax.axis_index("ch")
    x, y = ctx // SIDE, lax.rem(ctx, SIDE)
    z, core = ch // 2, lax.rem(ch, 2)

    def shifted(position, by):
        return lax.rem(position + by, SIDE)

    partners = [shifted(x, dx) * SIDE + shifted(y, dy) for dx, dy in ROUTES]
    other = (ctx, z * 2 + 1 - core)
    up = (ctx, shifted(z, 1) * 2 + core)
    down = (ctx, shifted(z, 3) * 2 + core)

    barrier = pltpu.get_barrier_semaphore()
    for partner in partners:
        pl.semaphore_signal(barrier, inc=1, device_id=(partner, ch), device_id_type=MESH)
    for device in (other, up, down):
        pl.semaphore_signal(barrier, inc=1, device_id=device, device_id_type=MESH)

    loads = []
    for i, (src, dst) in enumerate(((h_hbm, h), (v_hbm, v), (f1_hbm, f1), (m_hbm, m), (mb_hbm, mb), (f2_hbm, f2), (g_hbm, g), (bias_hbm, bias_ref))):
        load = pltpu.make_async_copy(src, dst, in_sem.at[i])
        load.start()
        loads.append(load)
    w_load = pltpu.make_async_copy(w_hbm, w, w_sem)
    w_load.start()

    low = lax.broadcasted_iota(jnp.int32, (ROWS, LANES), 1) < HALF
    loads[0].wait()
    loads[1].wait()
    for t in range(8):
        columns = slice(t * LANES, (t + 1) * LANES)
        values, taps = v[:, columns].astype(jnp.float32), h[:, columns]
        send[2 * t] = jnp.where(low, values, pltpu.roll(taps, HALF, 1)).astype(jnp.bfloat16)
        send[2 * t + 1] = jnp.where(low, pltpu.roll(values, HALF, 1), taps).astype(jnp.bfloat16)

    pl.semaphore_wait(barrier, len(ROUTES) + 3)
    copies = []
    for i, partner in enumerate(partners):
        copy = pltpu.make_async_remote_copy(
            send.at[partner], recv.at[ctx], s_sem.at[i], r_sem.at[i], device_id=(partner, ch), device_id_type=MESH)
        copy.start()
        copies.append(copy)
    recv[ctx] = send[ctx]
    for i in range(2, 6):
        loads[i].wait()
    for copy in copies:
        copy.wait()

    for k in range(ROWS // GROUP):
        rows = slice(k * GROUP, (k + 1) * GROUP)
        part = dot(f1[...], recv[:, rows, :].reshape(BLOCKS * GROUP, LANES))
        mid[:, :, rows, :] = part.astype(jnp.bfloat16).reshape(16, 2, GROUP, LANES)
    low_half = lax.broadcasted_iota(jnp.int32, (HALF, LANES), 1) < HALF
    for s in range(16):
        spectrum = dot(m[s], mid[s].reshape(2 * ROWS, LANES))
        real, imag = spectrum[:ROWS], spectrum[ROWS:]
        real2, imag2 = pltpu.roll(real, HALF, 1), pltpu.roll(imag, HALF, 1)
        rr, ii = real * real2, imag * imag2
        prod_real, prod_imag = rr - ii, real * imag2 + imag * real2
        if s == 0:
            top = lax.broadcasted_iota(jnp.int32, (ROWS, LANES), 0) == 0
            prod_real, prod_imag = jnp.where(top, rr, prod_real), jnp.where(top, ii, prod_imag)
        product = jnp.concatenate([prod_real, prod_imag], axis=0).astype(jnp.bfloat16)
        turned = dot(mb[s], product)
        for part in range(2):
            first, second = turned[part * ROWS:part * ROWS + HALF], turned[part * ROWS + HALF:(part + 1) * ROWS]
            back[s, part] = jnp.where(low_half, first, second).astype(jnp.bfloat16)
    for k in range(HALF // GROUP):
        rows = slice(k * GROUP, (k + 1) * GROUP)
        part = dot(f2[...], back[:, :, rows, :].reshape(2 * 16 * GROUP, LANES))
        bsend[:, rows, :] = part.astype(jnp.bfloat16).reshape(BLOCKS, GROUP, LANES)

    copies = []
    for i, partner in enumerate(partners):
        copy = pltpu.make_async_remote_copy(
            bsend.at[partner], brecv.at[ctx], bs_sem.at[i], br_sem.at[i], device_id=(partner, ch), device_id_type=MESH)
        copy.start()
        copies.append(copy)
    brecv[ctx] = bsend[ctx]
    loads[6].wait()
    loads[7].wait()
    for copy in copies:
        copy.wait()

    for t in range(8):
        columns = slice(t * LANES, (t + 1) * LANES)
        even, odd = brecv[2 * t].astype(jnp.float32), brecv[2 * t + 1].astype(jnp.float32)
        for part in range(2):
            rows = slice(part * HALF, (part + 1) * HALF)
            if part == 0:
                convolved = jnp.where(low_half, even, pltpu.roll(odd, HALF, 1))
            else:
                convolved = jnp.where(low_half, pltpu.roll(even, HALF, 1), odd)
            values = v[rows, columns].astype(jnp.float32)
            gate = g[rows, columns].astype(jnp.float32)
            gated[rows, columns] = ((convolved + bias_ref[0:1, columns] * values) * gate).astype(jnp.bfloat16)

    w_load.wait()

    def project(distance, part, to_core):
        start = (shifted(z, distance) * 2 + to_core) * 1024 + part * 512
        return dot(gated[...], w[:, pl.ds(pl.multiple_of(start, 512), 512)])

    def to_other(distance, part):
        i = 2 * distance + part
        psend[i] = project(distance, part, 1 - core).astype(jnp.bfloat16)
        copy = pltpu.make_async_remote_copy(
            psend.at[i], precv.at[i], ps_sem.at[i], pr_sem.at[i], device_id=other, device_id_type=MESH)
        copy.start()
        return copy

    def ring(i, device):
        copy = pltpu.make_async_remote_copy(
            ring_s.at[i], ring_r.at[i], rs_sem.at[i], rr_sem.at[i], device_id=device, device_id_type=MESH)
        copy.start()
        return copy

    pair = {}
    rings = {}

    def with_other(distance, part, own):
        pair[distance, part].wait_recv()
        return own + precv[2 * distance + part].astype(jnp.float32)

    for distance, part in ((2, 0), (2, 1), (1, 1), (3, 0)):
        pair[distance, part] = to_other(distance, part)
    for part in range(2):
        keep[part] = project(2, part, core)
    for part, device in ((0, up), (1, down)):
        ring_s[part] = with_other(2, part, keep[part]).astype(jnp.bfloat16)
        rings[part] = ring(part, device)
    for distance, part in ((1, 0), (3, 1)):
        pair[distance, part] = to_other(distance, part)
    keep[0], keep[1] = project(1, 1, core), project(3, 0, core)
    for i, distance, part, device in ((2, 1, 1, up), (3, 3, 0, down)):
        ring_s[i] = with_other(distance, part, keep[i - 2]).astype(jnp.bfloat16)
        rings[i] = ring(i, device)
    for part in range(2):
        pair[0, part] = to_other(0, part)
    relay[0], relay[1] = project(1, 0, core), project(3, 1, core)
    for part in range(2):
        keep[part] = project(0, part, core)
    for i, distance, part in ((0, 1, 0), (1, 3, 1)):
        relay[i] = with_other(distance, part, relay[i])
    for part in range(2):
        keep[part] = with_other(0, part, keep[part])
    for i, device in ((4, up), (5, down)):
        rings[i - 4].wait_recv()
        ring_s[i] = (relay[i - 4] + ring_r[i - 4].astype(jnp.float32)).astype(jnp.bfloat16)
        rings[i] = ring(i, device)
    for part, i in ((0, 3), (1, 2)):
        rings[i].wait_recv()
        keep[part] += ring_r[i].astype(jnp.float32)
    for part, i in ((0, 4), (1, 5)):
        rings[i].wait_recv()
        out_ref[:, part * 512:(part + 1) * 512] = keep[part] + ring_r[i].astype(jnp.float32)
    for copy in (*pair.values(), *rings.values()):
        copy.wait_send()


def on_device(keyed_values, gate_values, long_filter, skip_bias, out_weight):
    first, middle, middle_back, last = (jnp.asarray(t) for t in tables())
    bf, f32 = jnp.bfloat16, jnp.float32
    hbm = pl.BlockSpec(memory_space=pltpu.HBM)
    vmem = pl.BlockSpec(memory_space=pltpu.VMEM)
    dma = pltpu.SemaphoreType.DMA
    hops = len(ROUTES)
    return pl.pallas_call(
        kernel,
        out_shape=pltpu.VMEM((ROWS, 1024), f32),
        in_specs=[hbm, hbm, hbm, hbm, hbm, hbm, hbm, hbm, hbm],
        out_specs=vmem,
        scratch_shapes=[
            pltpu.VMEM((ROWS, 1024), bf),
            pltpu.VMEM((ROWS, 1024), bf),
            pltpu.VMEM((ROWS, 1024), f32),
            pltpu.VMEM((1, 1024), f32),
            pltpu.VMEM((1024, 8192), bf),
            pltpu.VMEM((512, 256), bf),
            pltpu.VMEM((16, 256, 256), bf),
            pltpu.VMEM((16, 256, 256), bf),
            pltpu.VMEM((256, 512), bf),
            pltpu.VMEM((BLOCKS, ROWS, LANES), bf),
            pltpu.VMEM((BLOCKS, ROWS, LANES), bf),
            pltpu.VMEM((16, 2, ROWS, LANES), bf),
            pltpu.VMEM((16, 2, HALF, LANES), bf),
            pltpu.VMEM((BLOCKS, HALF, LANES), bf),
            pltpu.VMEM((BLOCKS, HALF, LANES), bf),
            pltpu.VMEM((ROWS, 1024), bf),
            pltpu.VMEM((8, ROWS, 512), bf),
            pltpu.VMEM((8, ROWS, 512), bf),
            pltpu.VMEM((6, ROWS, 512), bf),
            pltpu.VMEM((6, ROWS, 512), bf),
            pltpu.VMEM((2, ROWS, 512), f32),
            pltpu.VMEM((2, ROWS, 512), f32),
            dma((8,)),
            dma,
            dma((hops,)),
            dma((hops,)),
            dma((hops,)),
            dma((hops,)),
            dma((8,)),
            dma((8,)),
            dma((6,)),
            dma((6,)),
        ],
        compiler_params=pltpu.CompilerParams(
            collective_id=0, has_side_effects=True, vmem_limit_bytes=60 << 20),
        cost_estimate=pl.CostEstimate(flops=3 << 30, bytes_accessed=24 << 20, transcendentals=0),
    )(keyed_values, gate_values, long_filter, skip_bias.reshape(1, 1024), out_weight, first, middle, middle_back, last)


def solution(mesh):
    return jax.shard_map(
        on_device,
        mesh=mesh,
        in_specs=(P("ctx", "ch"), P("ctx", "ch"), P("ctx", "ch"), P("ch"), P("ch", None)),
        out_specs=P("ctx", "ch"),
        check_vma=False,
    )
```

```python
import functools
import math

import jax
import jax.numpy as jnp
import ml_dtypes
import numpy as np
from jax import lax
from jax.experimental import pallas as pl
from jax.experimental.pallas import tpu as pltpu
from jax.sharding import PartitionSpec as P

MESH = pl.DeviceIdType.MESH
SIDE = 4
BLOCKS = 16
ROWS = 128
LANES = 128
HALF = 64
SPAN = 32
FULL = 2 * BLOCKS * ROWS
GROUP = 16
ROUTES = ((2, 2), (2, 1), (1, 2), (2, 3), (3, 2), (2, 0), (0, 2), (1, 1), (3, 3), (1, 3), (3, 1),
          (1, 0), (3, 0), (0, 1), (0, 3))


@functools.cache
def tables():
    a = np.arange(BLOCKS)
    forward = np.zeros((16, 2, BLOCKS))
    inverse = np.zeros((BLOCKS, 16, 2))
    for k1 in range(16):
        angle = 2 * math.pi * a * k1 / 32
        forward[k1, 0] = np.cos(angle)
        forward[k1, 1] = -np.sin(angle)
        inverse[:, k1, 0] = 2 * np.cos(angle)
        inverse[:, k1, 1] = -2 * np.sin(angle)
    forward[0, 1] = (-1.0) ** a
    inverse[:, 0, 0] = 1.0
    inverse[:, 0, 1] = (-1.0) ** a
    eye = np.eye(GROUP)
    first = np.kron(forward.reshape(32, BLOCKS), eye)
    last = np.kron(inverse.reshape(BLOCKS, 32) / 32, eye)
    b = np.arange(ROWS)
    middle = np.zeros((16, 256, 256))
    middle_back = np.zeros((16, 256, 256))
    for k1 in range(1, 16):
        angle = 2 * math.pi * np.outer(k1 + 32 * b, b) / FULL
        c, s = np.cos(angle), np.sin(angle)
        middle[k1] = np.block([[c, s], [-s, c]])
        middle_back[k1] = np.block([[c.T, -s.T], [s.T, c.T]]) / 128
    k2 = np.arange(64)
    angle = 2 * math.pi * np.outer(k2, b) / 128
    c, s = np.cos(angle), np.sin(angle)
    imag = -s
    imag[0] = (-1.0) ** b
    middle[0, 0:64, 0:128] = c
    middle[0, 128:192, 0:128] = imag
    weight = np.full((64, 1), 2.0)
    weight[0] = 1.0
    middle_back[0, 0:128, 0:64] = (weight * c).T / 128
    middle_back[0, 0:128, 128:192] = (weight * imag).T / 128
    angle = 2 * math.pi * np.outer(16 + 32 * k2, b) / FULL
    c, s = np.cos(angle), np.sin(angle)
    middle[0, 64:128, 128:256] = c
    middle[0, 192:256, 128:256] = -s
    middle_back[0, 128:256, 64:128] = 2 * c.T / 128
    middle_back[0, 128:256, 192:256] = -2 * s.T / 128
    return tuple(t.astype(ml_dtypes.bfloat16) for t in (first, middle, middle_back, last))


def dot(left, right):
    return jnp.dot(left, right, preferred_element_type=jnp.float32)


def kernel(v_hbm, g_hbm, h_hbm, bias_hbm, w_hbm, f1_hbm, m_hbm, mb_hbm, f2_hbm, out_ref,
           v, g, h, bias_ref, w, f1, m, mb, f2, send, recv, mid, back, bsend, brecv, gated, psend, precv, ring_s, ring_r,
           keep, relay, in_sem, w_sem, s_sem, r_sem, bs_sem, br_sem, ps_sem, pr_sem, rs_sem, rr_sem):
    ctx, ch = lax.axis_index("ctx"), lax.axis_index("ch")
    x, y = ctx // SIDE, lax.rem(ctx, SIDE)
    z, core = ch // 2, lax.rem(ch, 2)

    def shifted(position, by):
        return lax.rem(position + by, SIDE)

    partners = [shifted(x, dx) * SIDE + shifted(y, dy) for dx, dy in ROUTES]
    other = (ctx, z * 2 + 1 - core)
    up = (ctx, shifted(z, 1) * 2 + core)
    down = (ctx, shifted(z, 3) * 2 + core)
    up_crossed = (ctx, shifted(z, 1) * 2 + 1 - core)
    down_crossed = (ctx, shifted(z, 3) * 2 + 1 - core)

    barrier = pltpu.get_barrier_semaphore()
    for partner in partners:
        pl.semaphore_signal(barrier, inc=1, device_id=(partner, ch), device_id_type=MESH)
    for device in (up_crossed, down_crossed, up, down, other):
        pl.semaphore_signal(barrier, inc=1, device_id=device, device_id_type=MESH)

    loads = []
    for i, (src, dst) in enumerate(((h_hbm, h), (v_hbm, v), (f1_hbm, f1), (m_hbm, m), (mb_hbm, mb), (f2_hbm, f2), (g_hbm, g), (bias_hbm, bias_ref))):
        load = pltpu.make_async_copy(src, dst, in_sem.at[i])
        load.start()
        loads.append(load)
    w_load = pltpu.make_async_copy(w_hbm, w, w_sem)
    w_load.start()

    low = lax.broadcasted_iota(jnp.int32, (ROWS, LANES), 1) < HALF
    loads[0].wait()
    loads[1].wait()
    for t in range(8):
        columns = slice(t * LANES, (t + 1) * LANES)
        values, taps = v[:, columns].astype(jnp.float32), h[:, columns]
        send[2 * t] = jnp.where(low, values, pltpu.roll(taps, HALF, 1)).astype(jnp.bfloat16)
        send[2 * t + 1] = jnp.where(low, pltpu.roll(values, HALF, 1), taps).astype(jnp.bfloat16)

    pl.semaphore_wait(barrier, len(ROUTES) + 5)
    copies = []
    for i, partner in enumerate(partners):
        copy = pltpu.make_async_remote_copy(
            send.at[partner], recv.at[ctx], s_sem.at[i], r_sem.at[i], device_id=(partner, ch), device_id_type=MESH)
        copy.start()
        copies.append(copy)
    recv[ctx] = send[ctx]
    for i in range(2, 6):
        loads[i].wait()
    for copy in copies:
        copy.wait()

    for k in range(0, ROWS // GROUP, 2):
        both = [slice(e * GROUP, (e + 1) * GROUP) for e in (k, k + 1)]
        pair = [recv[:, rows, :].reshape(BLOCKS * GROUP, LANES) for rows in both]
        part = dot(f1[...], jnp.concatenate(pair, axis=1)).astype(jnp.bfloat16)
        for e, rows in enumerate(both):
            mid[:, :, rows, :] = part[:, e * LANES:(e + 1) * LANES].reshape(16, 2, GROUP, LANES)
    low_half = lax.broadcasted_iota(jnp.int32, (HALF, LANES), 1) < HALF
    for s0 in range(0, 16, 16):
        slots = range(s0, s0 + 16)
        spectra = [dot(m[s], mid[s].reshape(2 * ROWS, LANES)) for s in slots]
        products = []
        for s, spectrum in zip(slots, spectra):
            real, imag = spectrum[:ROWS], spectrum[ROWS:]
            real2, imag2 = pltpu.roll(real, HALF, 1), pltpu.roll(imag, HALF, 1)
            rr, ii = real * real2, imag * imag2
            prod_real, prod_imag = rr - ii, real * imag2 + imag * real2
            if s == 0:
                top = lax.broadcasted_iota(jnp.int32, (ROWS, LANES), 0) == 0
                prod_real, prod_imag = jnp.where(top, rr, prod_real), jnp.where(top, ii, prod_imag)
            products.append(jnp.concatenate([prod_real, prod_imag], axis=0).astype(jnp.bfloat16))
        for s, product in zip(slots, products):
            turned = dot(mb[s], product)
            for part in range(2):
                first, second = turned[part * ROWS:part * ROWS + HALF], turned[part * ROWS + HALF:(part + 1) * ROWS]
                back[s, part] = jnp.where(low_half, first, second).astype(jnp.bfloat16)
    returned = []
    for q in range(2):
        both = [slice(e * GROUP, (e + 1) * GROUP) for e in (2 * q, 2 * q + 1)]
        pair = [back[:, :, rows, :].reshape(2 * 16 * GROUP, LANES) for rows in both]
        part = dot(f2[...], jnp.concatenate(pair, axis=1)).astype(jnp.bfloat16)
        for e in range(2):
            bsend[q, :, e * GROUP:(e + 1) * GROUP, :] = part[:, e * LANES:(e + 1) * LANES].reshape(BLOCKS, GROUP, LANES)
        copies = []
        for i, partner in enumerate(partners):
            copy = pltpu.make_async_remote_copy(
                bsend.at[q, partner], brecv.at[q, ctx], bs_sem.at[q, i], br_sem.at[q, i],
                device_id=(partner, ch), device_id_type=MESH)
            copy.start()
            copies.append(copy)
        brecv[q, ctx] = bsend[q, ctx]
        returned.append(copies)
    loads[6].wait()
    loads[7].wait()
    w_load.wait()
    def gate(q):
        mask = low_half[:SPAN]
        for t in range(8):
            columns = slice(t * LANES, (t + 1) * LANES)
            even, odd = brecv[q, 2 * t].astype(jnp.float32), brecv[q, 2 * t + 1].astype(jnp.float32)
            for part in range(2):
                rows = slice(part * HALF + q * SPAN, part * HALF + (q + 1) * SPAN)
                if part == 0:
                    convolved = jnp.where(mask, even, pltpu.roll(odd, HALF, 1))
                else:
                    convolved = jnp.where(mask, pltpu.roll(even, HALF, 1), odd)
                values = v[rows, columns].astype(jnp.float32)
                gates = g[rows, columns].astype(jnp.float32)
                total = ((convolved + bias_ref[0:1, columns] * values) * gates).astype(jnp.bfloat16)
                gated[q * HALF + part * SPAN:q * HALF + (part + 1) * SPAN, columns] = total

    def project(distance, part, to_core, rows=slice(0, ROWS)):
        start = (shifted(z, distance) * 2 + to_core) * 1024 + part * 512
        return dot(gated[rows, :], w[:, pl.ds(pl.multiple_of(start, 512), 512)])

    first_rows, last_rows = slice(0, HALF), slice(HALF, ROWS)
    everything = slice(0, ROWS)

    def to_other(distance, part, rows=everything):
        i = 2 * distance + part
        psend[i, rows, :] = project(distance, part, 1 - core, rows).astype(jnp.bfloat16)
        copy = pltpu.make_async_remote_copy(
            psend.at[i, rows], precv.at[i, rows], ps_sem.at[i], pr_sem.at[i], device_id=other, device_id_type=MESH)
        copy.start()
        pair[distance, part] = copy

    def with_other(distance, part, own, rows=everything):
        pair[distance, part].wait_recv()
        return own + precv[2 * distance + part, rows, :].astype(jnp.float32)

    def ring(i, device, rows=everything):
        copy = pltpu.make_async_remote_copy(
            ring_s.at[i, rows], ring_r.at[i, rows], rs_sem.at[i], rr_sem.at[i], device_id=device, device_id_type=MESH)
        copy.start()
        rings[i] = copy

    pair = {}
    rings = {}

    for copy in returned[0]:
        copy.wait_recv()
    gate(0)
    for i, distance, part, to_core, device in (
            (6, 1, 1, core, up), (7, 3, 0, core, down), (8, 1, 1, 1 - core, up_crossed), (9, 3, 0, 1 - core, down_crossed)):
        ring_s[i, first_rows, :] = project(distance, part, to_core, first_rows).astype(jnp.bfloat16)
        ring(i, device, first_rows)
    for copy in returned[1]:
        copy.wait_recv()
    gate(1)
    for distance, part in ((2, 0), (2, 1)):
        to_other(distance, part)
    for distance, part in ((1, 1), (3, 0)):
        to_other(distance, part, last_rows)
    for part in range(2):
        keep[part] = project(2, part, core)
    for part, device in ((0, up), (1, down)):
        ring_s[part] = with_other(2, part, keep[part]).astype(jnp.bfloat16)
        ring(part, device)
    for distance, part in ((1, 0), (3, 1)):
        to_other(distance, part)
    for i, distance, part in ((0, 1, 1), (1, 3, 0)):
        keep[i, last_rows, :] = project(distance, part, core, last_rows)
    for i, distance, part, device in ((2, 1, 1, up), (3, 3, 0, down)):
        ring_s[i, last_rows, :] = with_other(distance, part, keep[i - 2, last_rows, :], last_rows).astype(jnp.bfloat16)
        ring(i, device, last_rows)
    for part in range(2):
        to_other(0, part)
    relay[0], relay[1] = project(1, 0, core), project(3, 1, core)
    for part in range(2):
        keep[part] = project(0, part, core)
    for i, distance, part in ((0, 1, 0), (1, 3, 1)):
        relay[i] = with_other(distance, part, relay[i])
    for part in range(2):
        keep[part] = with_other(0, part, keep[part])
    for i, device in ((4, up), (5, down)):
        rings[i - 4].wait_recv()
        ring_s[i] = (relay[i - 4] + ring_r[i - 4].astype(jnp.float32)).astype(jnp.bfloat16)
        ring(i, device)
    for part, slots in ((0, (7, 9, 3)), (1, (6, 8, 2))):
        for i in slots:
            rows = last_rows if i < 4 else first_rows
            rings[i].wait_recv()
            keep[part, rows, :] += ring_r[i, rows, :].astype(jnp.float32)
    for part, i in ((0, 4), (1, 5)):
        rings[i].wait_recv()
        total = keep[part] + ring_r[i].astype(jnp.float32)
        for q in range(2):
            for half in range(2):
                token, row = half * HALF + q * SPAN, q * HALF + half * SPAN
                out_ref[token:token + SPAN, part * 512:(part + 1) * 512] = total[row:row + SPAN]
    for copies in (*returned, pair.values(), rings.values()):
        for copy in copies:
            copy.wait_send()


def on_device(keyed_values, gate_values, long_filter, skip_bias, out_weight):
    first, middle, middle_back, last = (jnp.asarray(t) for t in tables())
    bf, f32 = jnp.bfloat16, jnp.float32
    hbm = pl.BlockSpec(memory_space=pltpu.HBM)
    vmem = pl.BlockSpec(memory_space=pltpu.VMEM)
    dma = pltpu.SemaphoreType.DMA
    hops = len(ROUTES)
    return pl.pallas_call(
        kernel,
        out_shape=pltpu.VMEM((ROWS, 1024), f32),
        in_specs=[hbm, hbm, hbm, hbm, hbm, hbm, hbm, hbm, hbm],
        out_specs=vmem,
        scratch_shapes=[
            pltpu.VMEM((ROWS, 1024), bf),
            pltpu.VMEM((ROWS, 1024), bf),
            pltpu.VMEM((ROWS, 1024), f32),
            pltpu.VMEM((1, 1024), f32),
            pltpu.VMEM((1024, 8192), bf),
            pltpu.VMEM((512, 256), bf),
            pltpu.VMEM((16, 256, 256), bf),
            pltpu.VMEM((16, 256, 256), bf),
            pltpu.VMEM((256, 512), bf),
            pltpu.VMEM((BLOCKS, ROWS, LANES), bf),
            pltpu.VMEM((BLOCKS, ROWS, LANES), bf),
            pltpu.VMEM((16, 2, ROWS, LANES), bf),
            pltpu.VMEM((16, 2, HALF, LANES), bf),
            pltpu.VMEM((2, BLOCKS, SPAN, LANES), bf),
            pltpu.VMEM((2, BLOCKS, SPAN, LANES), bf),
            pltpu.VMEM((ROWS, 1024), bf),
            pltpu.VMEM((8, ROWS, 512), bf),
            pltpu.VMEM((8, ROWS, 512), bf),
            pltpu.VMEM((10, ROWS, 512), bf),
            pltpu.VMEM((10, ROWS, 512), bf),
            pltpu.VMEM((2, ROWS, 512), f32),
            pltpu.VMEM((2, ROWS, 512), f32),
            dma((8,)),
            dma,
            dma((hops,)),
            dma((hops,)),
            dma((2, hops)),
            dma((2, hops)),
            dma((8,)),
            dma((8,)),
            dma((10,)),
            dma((10,)),
        ],
        compiler_params=pltpu.CompilerParams(
            collective_id=0, has_side_effects=True, vmem_limit_bytes=60 << 20),
        cost_estimate=pl.CostEstimate(flops=3 << 30, bytes_accessed=24 << 20, transcendentals=0),
    )(keyed_values, gate_values, long_filter, skip_bias.reshape(1, 1024), out_weight, first, middle, middle_back, last)


def solution(mesh):
    return jax.shard_map(
        on_device,
        mesh=mesh,
        in_specs=(P("ctx", "ch"), P("ctx", "ch"), P("ctx", "ch"), P("ch"), P("ch", None)),
        out_specs=P("ctx", "ch"),
        check_vma=False,
    )
```

```python
import functools
import math

import jax
import jax.numpy as jnp
import ml_dtypes
import numpy as np
from jax import lax
from jax.experimental import pallas as pl
from jax.experimental.pallas import tpu as pltpu
from jax.sharding import PartitionSpec as P

MESH = pl.DeviceIdType.MESH
SIDE = 4
BLOCKS = 16
ROWS = 128
LANES = 128
HALF = 64
SPAN = 32
FULL = 2 * BLOCKS * ROWS
GROUP = 16
ROUTES = ((2, 2), (2, 1), (1, 2), (2, 3), (3, 2), (2, 0), (0, 2), (1, 1), (3, 3), (1, 3), (3, 1),
          (1, 0), (3, 0), (0, 1), (0, 3))


@functools.cache
def tables():
    a = np.arange(BLOCKS)
    forward = np.zeros((16, 2, BLOCKS))
    inverse = np.zeros((BLOCKS, 16, 2))
    for k1 in range(16):
        angle = 2 * math.pi * a * k1 / 32
        forward[k1, 0] = np.cos(angle)
        forward[k1, 1] = -np.sin(angle)
        inverse[:, k1, 0] = 2 * np.cos(angle)
        inverse[:, k1, 1] = -2 * np.sin(angle)
    forward[0, 1] = (-1.0) ** a
    inverse[:, 0, 0] = 1.0
    inverse[:, 0, 1] = (-1.0) ** a
    eye = np.eye(GROUP)
    first = np.kron(forward.reshape(32, BLOCKS), eye)
    last = np.kron(inverse.reshape(BLOCKS, 32) / 32, eye)
    b = np.arange(ROWS)
    middle = np.zeros((16, 256, 256))
    middle_back = np.zeros((16, 256, 256))
    for k1 in range(1, 16):
        angle = 2 * math.pi * np.outer(k1 + 32 * b, b) / FULL
        c, s = np.cos(angle), np.sin(angle)
        middle[k1] = np.block([[c, s], [-s, c]])
        middle_back[k1] = np.block([[c.T, -s.T], [s.T, c.T]]) / 128
    k2 = np.arange(64)
    angle = 2 * math.pi * np.outer(k2, b) / 128
    c, s = np.cos(angle), np.sin(angle)
    imag = -s
    imag[0] = (-1.0) ** b
    middle[0, 0:64, 0:128] = c
    middle[0, 128:192, 0:128] = imag
    weight = np.full((64, 1), 2.0)
    weight[0] = 1.0
    middle_back[0, 0:128, 0:64] = (weight * c).T / 128
    middle_back[0, 0:128, 128:192] = (weight * imag).T / 128
    angle = 2 * math.pi * np.outer(16 + 32 * k2, b) / FULL
    c, s = np.cos(angle), np.sin(angle)
    middle[0, 64:128, 128:256] = c
    middle[0, 192:256, 128:256] = -s
    middle_back[0, 128:256, 64:128] = 2 * c.T / 128
    middle_back[0, 128:256, 192:256] = -2 * s.T / 128
    return tuple(t.astype(ml_dtypes.bfloat16) for t in (first, middle, middle_back, last))


def dot(left, right):
    return jnp.dot(left, right, preferred_element_type=jnp.float32)


def kernel(v_hbm, g_hbm, h_hbm, bias_hbm, w_hbm, f1_hbm, m_hbm, mb_hbm, f2_hbm, out_ref,
           v, g, h, bias_ref, w, f1, m, mb, f2, send, recv, mid, back, bsend, brecv, gated, psend, precv, ring_s, ring_r,
           keep, relay, in_sem, w_sem, s_sem, r_sem, bs_sem, br_sem, ps_sem, pr_sem, rs_sem, rr_sem):
    ctx, ch = lax.axis_index("ctx"), lax.axis_index("ch")
    x, y = ctx // SIDE, lax.rem(ctx, SIDE)
    z, core = ch // 2, lax.rem(ch, 2)

    def shifted(position, by):
        return lax.rem(position + by, SIDE)

    partners = [shifted(x, dx) * SIDE + shifted(y, dy) for dx, dy in ROUTES]
    other = (ctx, z * 2 + 1 - core)
    up = (ctx, shifted(z, 1) * 2 + core)
    down = (ctx, shifted(z, 3) * 2 + core)
    up_crossed = (ctx, shifted(z, 1) * 2 + 1 - core)
    down_crossed = (ctx, shifted(z, 3) * 2 + 1 - core)

    barrier = pltpu.get_barrier_semaphore()
    for partner in partners:
        pl.semaphore_signal(barrier, inc=1, device_id=(partner, ch), device_id_type=MESH)
    for device in (up_crossed, down_crossed, up, down, other):
        pl.semaphore_signal(barrier, inc=1, device_id=device, device_id_type=MESH)

    loads = []
    for i, (src, dst) in enumerate(((h_hbm, h), (v_hbm, v), (f1_hbm, f1), (m_hbm, m), (mb_hbm, mb), (f2_hbm, f2), (g_hbm, g), (bias_hbm, bias_ref))):
        load = pltpu.make_async_copy(src, dst, in_sem.at[i])
        load.start()
        loads.append(load)
    w_load = pltpu.make_async_copy(w_hbm, w, w_sem)
    w_load.start()

    low = lax.broadcasted_iota(jnp.int32, (ROWS, LANES), 1) < HALF
    loads[0].wait()
    loads[1].wait()
    for q in range(2):
        rows, mask = slice(q * HALF, (q + 1) * HALF), low[:HALF]
        for t in range(8):
            columns = slice(t * LANES, (t + 1) * LANES)
            values, taps = v[rows, columns].astype(jnp.float32), h[rows, columns]
            send[q, 2 * t] = jnp.where(mask, values, pltpu.roll(taps, HALF, 1)).astype(jnp.bfloat16)
            send[q, 2 * t + 1] = jnp.where(mask, pltpu.roll(values, HALF, 1), taps).astype(jnp.bfloat16)

    pl.semaphore_wait(barrier, len(ROUTES) + 5)
    forth = []
    for q in range(2):
        copies = []
        for i, partner in enumerate(partners):
            copy = pltpu.make_async_remote_copy(
                send.at[q, partner], recv.at[q, ctx], s_sem.at[q, i], r_sem.at[q, i],
                device_id=(partner, ch), device_id_type=MESH)
            copy.start()
            copies.append(copy)
        forth.append(copies)
    for q in range(2):
        recv[q, ctx] = send[q, ctx]
    for i in range(2, 6):
        loads[i].wait()

    for q in range(2):
        for copy in forth[q]:
            copy.wait_recv()
        for k in range(0, HALF // GROUP, 2):
            both = [slice(e * GROUP, (e + 1) * GROUP) for e in (k, k + 1)]
            pair = [recv[q, :, rows, :].reshape(BLOCKS * GROUP, LANES) for rows in both]
            part = dot(f1[...], jnp.concatenate(pair, axis=1)).astype(jnp.bfloat16)
            for e in range(2):
                start = q * HALF + (k + e) * GROUP
                mid[:, :, start:start + GROUP, :] = part[:, e * LANES:(e + 1) * LANES].reshape(16, 2, GROUP, LANES)
    low_half = lax.broadcasted_iota(jnp.int32, (HALF, LANES), 1) < HALF
    for s0 in range(0, 16, 16):
        slots = range(s0, s0 + 16)
        spectra = [dot(m[s], mid[s].reshape(2 * ROWS, LANES)) for s in slots]
        products = []
        for s, spectrum in zip(slots, spectra):
            real, imag = spectrum[:ROWS], spectrum[ROWS:]
            real2, imag2 = pltpu.roll(real, HALF, 1), pltpu.roll(imag, HALF, 1)
            rr, ii = real * real2, imag * imag2
            prod_real, prod_imag = rr - ii, real * imag2 + imag * real2
            if s == 0:
                top = lax.broadcasted_iota(jnp.int32, (ROWS, LANES), 0) == 0
                prod_real, prod_imag = jnp.where(top, rr, prod_real), jnp.where(top, ii, prod_imag)
            products.append(jnp.concatenate([prod_real, prod_imag], axis=0).astype(jnp.bfloat16))
        for s, product in zip(slots, products):
            turned = dot(mb[s], product)
            for part in range(2):
                first, second = turned[part * ROWS:part * ROWS + HALF], turned[part * ROWS + HALF:(part + 1) * ROWS]
                back[s, part] = jnp.where(low_half, first, second).astype(jnp.bfloat16)
    returned = []
    for q in range(2):
        both = [slice(e * GROUP, (e + 1) * GROUP) for e in (2 * q, 2 * q + 1)]
        pair = [back[:, :, rows, :].reshape(2 * 16 * GROUP, LANES) for rows in both]
        part = dot(f2[...], jnp.concatenate(pair, axis=1)).astype(jnp.bfloat16)
        for e in range(2):
            bsend[q, :, e * GROUP:(e + 1) * GROUP, :] = part[:, e * LANES:(e + 1) * LANES].reshape(BLOCKS, GROUP, LANES)
        copies = []
        for i, partner in enumerate(partners):
            copy = pltpu.make_async_remote_copy(
                bsend.at[q, partner], brecv.at[q, ctx], bs_sem.at[q, i], br_sem.at[q, i],
                device_id=(partner, ch), device_id_type=MESH)
            copy.start()
            copies.append(copy)
        brecv[q, ctx] = bsend[q, ctx]
        returned.append(copies)
    loads[6].wait()
    loads[7].wait()
    w_load.wait()
    def gate(q):
        mask = low_half[:SPAN]
        for t in range(8):
            columns = slice(t * LANES, (t + 1) * LANES)
            even, odd = brecv[q, 2 * t].astype(jnp.float32), brecv[q, 2 * t + 1].astype(jnp.float32)
            for part in range(2):
                rows = slice(part * HALF + q * SPAN, part * HALF + (q + 1) * SPAN)
                if part == 0:
                    convolved = jnp.where(mask, even, pltpu.roll(odd, HALF, 1))
                else:
                    convolved = jnp.where(mask, pltpu.roll(even, HALF, 1), odd)
                values = v[rows, columns].astype(jnp.float32)
                gates = g[rows, columns].astype(jnp.float32)
                total = ((convolved + bias_ref[0:1, columns] * values) * gates).astype(jnp.bfloat16)
                gated[q * HALF + part * SPAN:q * HALF + (part + 1) * SPAN, columns] = total

    def project(distance, part, to_core, rows=slice(0, ROWS)):
        start = (shifted(z, distance) * 2 + to_core) * 1024 + part * 512
        return dot(gated[rows, :], w[:, pl.ds(pl.multiple_of(start, 512), 512)])

    first_rows, last_rows = slice(0, HALF), slice(HALF, ROWS)
    everything = slice(0, ROWS)

    def to_other(distance, part, rows=everything):
        i = 2 * distance + part
        psend[i, rows, :] = project(distance, part, 1 - core, rows).astype(jnp.bfloat16)
        copy = pltpu.make_async_remote_copy(
            psend.at[i, rows], precv.at[i, rows], ps_sem.at[i], pr_sem.at[i], device_id=other, device_id_type=MESH)
        copy.start()
        pair[distance, part] = copy

    def with_other(distance, part, own, rows=everything):
        pair[distance, part].wait_recv()
        return own + precv[2 * distance + part, rows, :].astype(jnp.float32)

    def ring(i, device, rows=everything):
        copy = pltpu.make_async_remote_copy(
            ring_s.at[i, rows], ring_r.at[i, rows], rs_sem.at[i], rr_sem.at[i], device_id=device, device_id_type=MESH)
        copy.start()
        rings[i] = copy

    pair = {}
    rings = {}

    for copy in returned[0]:
        copy.wait_recv()
    gate(0)
    for i, distance, part, to_core, device in (
            (6, 1, 1, core, up), (7, 3, 0, core, down), (8, 1, 1, 1 - core, up_crossed), (9, 3, 0, 1 - core, down_crossed)):
        ring_s[i, first_rows, :] = project(distance, part, to_core, first_rows).astype(jnp.bfloat16)
        ring(i, device, first_rows)
    for copy in returned[1]:
        copy.wait_recv()
    gate(1)
    for distance, part in ((2, 0), (2, 1)):
        to_other(distance, part)
    for distance, part in ((1, 1), (3, 0)):
        to_other(distance, part, last_rows)
    for part in range(2):
        keep[part] = project(2, part, core)
    for part, device in ((0, up), (1, down)):
        ring_s[part] = with_other(2, part, keep[part]).astype(jnp.bfloat16)
        ring(part, device)
    for distance, part in ((1, 0), (3, 1)):
        to_other(distance, part)
    for i, distance, part in ((0, 1, 1), (1, 3, 0)):
        keep[i, last_rows, :] = project(distance, part, core, last_rows)
    for i, distance, part, device in ((2, 1, 1, up), (3, 3, 0, down)):
        ring_s[i, last_rows, :] = with_other(distance, part, keep[i - 2, last_rows, :], last_rows).astype(jnp.bfloat16)
        ring(i, device, last_rows)
    for part in range(2):
        to_other(0, part)
    relay[0], relay[1] = project(1, 0, core), project(3, 1, core)
    for part in range(2):
        keep[part] = project(0, part, core)
    for i, distance, part in ((0, 1, 0), (1, 3, 1)):
        relay[i] = with_other(distance, part, relay[i])
    for part in range(2):
        keep[part] = with_other(0, part, keep[part])
    for i, device in ((4, up), (5, down)):
        rings[i - 4].wait_recv()
        ring_s[i] = (relay[i - 4] + ring_r[i - 4].astype(jnp.float32)).astype(jnp.bfloat16)
        ring(i, device)
    for part, slots in ((0, (7, 9, 3)), (1, (6, 8, 2))):
        for i in slots:
            rows = last_rows if i < 4 else first_rows
            rings[i].wait_recv()
            keep[part, rows, :] += ring_r[i, rows, :].astype(jnp.float32)
    for part, i in ((0, 4), (1, 5)):
        rings[i].wait_recv()
        total = keep[part] + ring_r[i].astype(jnp.float32)
        for q in range(2):
            for half in range(2):
                token, row = half * HALF + q * SPAN, q * HALF + half * SPAN
                out_ref[token:token + SPAN, part * 512:(part + 1) * 512] = total[row:row + SPAN]
    for copies in (*forth, *returned, pair.values(), rings.values()):
        for copy in copies:
            copy.wait_send()


def on_device(keyed_values, gate_values, long_filter, skip_bias, out_weight):
    first, middle, middle_back, last = (jnp.asarray(t) for t in tables())
    bf, f32 = jnp.bfloat16, jnp.float32
    hbm = pl.BlockSpec(memory_space=pltpu.HBM)
    vmem = pl.BlockSpec(memory_space=pltpu.VMEM)
    dma = pltpu.SemaphoreType.DMA
    hops = len(ROUTES)
    return pl.pallas_call(
        kernel,
        out_shape=pltpu.VMEM((ROWS, 1024), f32),
        in_specs=[hbm, hbm, hbm, hbm, hbm, hbm, hbm, hbm, hbm],
        out_specs=vmem,
        scratch_shapes=[
            pltpu.VMEM((ROWS, 1024), bf),
            pltpu.VMEM((ROWS, 1024), bf),
            pltpu.VMEM((ROWS, 1024), f32),
            pltpu.VMEM((1, 1024), f32),
            pltpu.VMEM((1024, 8192), bf),
            pltpu.VMEM((512, 256), bf),
            pltpu.VMEM((16, 256, 256), bf),
            pltpu.VMEM((16, 256, 256), bf),
            pltpu.VMEM((256, 512), bf),
            pltpu.VMEM((2, BLOCKS, HALF, LANES), bf),
            pltpu.VMEM((2, BLOCKS, HALF, LANES), bf),
            pltpu.VMEM((16, 2, ROWS, LANES), bf),
            pltpu.VMEM((16, 2, HALF, LANES), bf),
            pltpu.VMEM((2, BLOCKS, SPAN, LANES), bf),
            pltpu.VMEM((2, BLOCKS, SPAN, LANES), bf),
            pltpu.VMEM((ROWS, 1024), bf),
            pltpu.VMEM((8, ROWS, 512), bf),
            pltpu.VMEM((8, ROWS, 512), bf),
            pltpu.VMEM((10, ROWS, 512), bf),
            pltpu.VMEM((10, ROWS, 512), bf),
            pltpu.VMEM((2, ROWS, 512), f32),
            pltpu.VMEM((2, ROWS, 512), f32),
            dma((8,)),
            dma,
            dma((2, hops)),
            dma((2, hops)),
            dma((2, hops)),
            dma((2, hops)),
            dma((8,)),
            dma((8,)),
            dma((10,)),
            dma((10,)),
        ],
        compiler_params=pltpu.CompilerParams(
            collective_id=0, has_side_effects=True, vmem_limit_bytes=60 << 20),
        cost_estimate=pl.CostEstimate(flops=3 << 30, bytes_accessed=24 << 20, transcendentals=0),
    )(keyed_values, gate_values, long_filter, skip_bias.reshape(1, 1024), out_weight, first, middle, middle_back, last)


def solution(mesh):
    return jax.shard_map(
        on_device,
        mesh=mesh,
        in_specs=(P("ctx", "ch"), P("ctx", "ch"), P("ctx", "ch"), P("ch"), P("ch", None)),
        out_specs=P("ctx", "ch"),
        check_vma=False,
    )
```

```python
import functools
import math

import jax
import jax.numpy as jnp
import ml_dtypes
import numpy as np
from jax import lax
from jax.experimental import pallas as pl
from jax.experimental.pallas import tpu as pltpu
from jax.sharding import PartitionSpec as P

MESH = pl.DeviceIdType.MESH
SIDE = 4
BLOCKS = 16
ROWS = 128
LANES = 128
HALF = 64
SPAN = 32
FULL = 2 * BLOCKS * ROWS
GROUP = 16
ROUTES = ((2, 2), (2, 1), (1, 2), (2, 3), (3, 2), (2, 0), (0, 2), (1, 1), (3, 3), (1, 3), (3, 1),
          (1, 0), (3, 0), (0, 1), (0, 3))


@functools.cache
def tables():
    a = np.arange(BLOCKS)
    forward = np.zeros((16, 2, BLOCKS))
    inverse = np.zeros((BLOCKS, 16, 2))
    for k1 in range(16):
        angle = 2 * math.pi * a * k1 / 32
        forward[k1, 0] = np.cos(angle)
        forward[k1, 1] = -np.sin(angle)
        inverse[:, k1, 0] = 2 * np.cos(angle)
        inverse[:, k1, 1] = -2 * np.sin(angle)
    forward[0, 1] = (-1.0) ** a
    inverse[:, 0, 0] = 1.0
    inverse[:, 0, 1] = (-1.0) ** a
    eye = np.eye(GROUP)
    first = np.kron(forward.reshape(32, BLOCKS), eye)
    last = np.kron(inverse.reshape(BLOCKS, 32) / 32, eye)
    b = np.arange(ROWS)
    middle = np.zeros((16, 256, 256))
    middle_back = np.zeros((16, 256, 256))
    for k1 in range(1, 16):
        angle = 2 * math.pi * np.outer(k1 + 32 * b, b) / FULL
        c, s = np.cos(angle), np.sin(angle)
        middle[k1] = np.block([[c, s], [-s, c]])
        middle_back[k1] = np.block([[c.T, -s.T], [s.T, c.T]]) / 128
    k2 = np.arange(64)
    angle = 2 * math.pi * np.outer(k2, b) / 128
    c, s = np.cos(angle), np.sin(angle)
    imag = -s
    imag[0] = (-1.0) ** b
    middle[0, 0:64, 0:128] = c
    middle[0, 128:192, 0:128] = imag
    weight = np.full((64, 1), 2.0)
    weight[0] = 1.0
    middle_back[0, 0:128, 0:64] = (weight * c).T / 128
    middle_back[0, 0:128, 128:192] = (weight * imag).T / 128
    angle = 2 * math.pi * np.outer(16 + 32 * k2, b) / FULL
    c, s = np.cos(angle), np.sin(angle)
    middle[0, 64:128, 128:256] = c
    middle[0, 192:256, 128:256] = -s
    middle_back[0, 128:256, 64:128] = 2 * c.T / 128
    middle_back[0, 128:256, 192:256] = -2 * s.T / 128
    return tuple(t.astype(ml_dtypes.bfloat16) for t in (first, middle, middle_back, last))


def dot(left, right):
    return jnp.dot(left, right, preferred_element_type=jnp.float32)


def kernel(v_hbm, g_hbm, h_hbm, bias_hbm, w_hbm, f1_hbm, m_hbm, mb_hbm, f2_hbm, out_ref,
           v, g, h, bias_ref, w, f1, m, mb, f2, send, recv, mid, back, bsend, brecv, gated, psend, precv, ring_s, ring_r,
           keep, relay, in_sem, w_sem, s_sem, r_sem, bs_sem, br_sem, ps_sem, pr_sem, rs_sem, rr_sem):
    ctx, ch = lax.axis_index("ctx"), lax.axis_index("ch")
    x, y = ctx // SIDE, lax.rem(ctx, SIDE)
    z, core = ch // 2, lax.rem(ch, 2)

    def shifted(position, by):
        return lax.rem(position + by, SIDE)

    partners = [shifted(x, dx) * SIDE + shifted(y, dy) for dx, dy in ROUTES]
    other = (ctx, z * 2 + 1 - core)
    up = (ctx, shifted(z, 1) * 2 + core)
    down = (ctx, shifted(z, 3) * 2 + core)
    up_crossed = (ctx, shifted(z, 1) * 2 + 1 - core)
    down_crossed = (ctx, shifted(z, 3) * 2 + 1 - core)

    barrier = pltpu.get_barrier_semaphore()
    for partner in partners:
        pl.semaphore_signal(barrier, inc=1, device_id=(partner, ch), device_id_type=MESH)
    for device in (up_crossed, down_crossed, up, down, other):
        pl.semaphore_signal(barrier, inc=1, device_id=device, device_id_type=MESH)

    loads = []
    for i, (src, dst) in enumerate(((h_hbm, h), (v_hbm, v), (f1_hbm, f1), (m_hbm, m), (mb_hbm, mb), (f2_hbm, f2), (g_hbm, g), (bias_hbm, bias_ref))):
        load = pltpu.make_async_copy(src, dst, in_sem.at[i])
        load.start()
        loads.append(load)
    w_load = pltpu.make_async_copy(w_hbm, w, w_sem)
    w_load.start()

    low = lax.broadcasted_iota(jnp.int32, (ROWS, LANES), 1) < HALF
    loads[0].wait()
    loads[1].wait()
    for t in range(8):
        columns = slice(t * LANES, (t + 1) * LANES)
        values, taps = v[:, columns].astype(jnp.float32), h[:, columns]
        send[2 * t] = jnp.where(low, values, pltpu.roll(taps, HALF, 1)).astype(jnp.bfloat16)
        send[2 * t + 1] = jnp.where(low, pltpu.roll(values, HALF, 1), taps).astype(jnp.bfloat16)

    pl.semaphore_wait(barrier, len(ROUTES) + 5)
    copies = []
    for i, partner in enumerate(partners):
        copy = pltpu.make_async_remote_copy(
            send.at[partner], recv.at[ctx], s_sem.at[i], r_sem.at[i], device_id=(partner, ch), device_id_type=MESH)
        copy.start()
        copies.append(copy)
    recv[ctx] = send[ctx]
    for i in range(2, 6):
        loads[i].wait()
    for copy in copies:
        copy.wait()

    for k in range(0, ROWS // GROUP, 2):
        both = [slice(e * GROUP, (e + 1) * GROUP) for e in (k, k + 1)]
        pair = [recv[:, rows, :].reshape(BLOCKS * GROUP, LANES) for rows in both]
        part = dot(f1[...], jnp.concatenate(pair, axis=1)).astype(jnp.bfloat16)
        for e, rows in enumerate(both):
            mid[:, :, rows, :] = part[:, e * LANES:(e + 1) * LANES].reshape(16, 2, GROUP, LANES)
    low_half = lax.broadcasted_iota(jnp.int32, (HALF, LANES), 1) < HALF
    for s0 in range(0, 16, 16):
        slots = range(s0, s0 + 16)
        spectra = [dot(m[s], mid[s].reshape(2 * ROWS, LANES)) for s in slots]
        products = []
        for s, spectrum in zip(slots, spectra):
            real, imag = spectrum[:ROWS], spectrum[ROWS:]
            real2, imag2 = pltpu.roll(real, HALF, 1), pltpu.roll(imag, HALF, 1)
            rr, ii = real * real2, imag * imag2
            prod_real, prod_imag = rr - ii, real * imag2 + imag * real2
            if s == 0:
                top = lax.broadcasted_iota(jnp.int32, (ROWS, LANES), 0) == 0
                prod_real, prod_imag = jnp.where(top, rr, prod_real), jnp.where(top, ii, prod_imag)
            products.append(jnp.concatenate([prod_real, prod_imag], axis=0).astype(jnp.bfloat16))
        for s, product in zip(slots, products):
            turned = dot(mb[s], product)
            for part in range(2):
                first, second = turned[part * ROWS:part * ROWS + HALF], turned[part * ROWS + HALF:(part + 1) * ROWS]
                back[s, part] = jnp.where(low_half, first, second).astype(jnp.bfloat16)
    returned = []
    for q in range(2):
        both = [slice(e * GROUP, (e + 1) * GROUP) for e in (2 * q, 2 * q + 1)]
        pair = [back[:, :, rows, :].reshape(2 * 16 * GROUP, LANES) for rows in both]
        part = dot(f2[...], jnp.concatenate(pair, axis=1)).astype(jnp.bfloat16)
        for e in range(2):
            bsend[q, :, e * GROUP:(e + 1) * GROUP, :] = part[:, e * LANES:(e + 1) * LANES].reshape(BLOCKS, GROUP, LANES)
        copies = []
        for i, partner in enumerate(partners):
            copy = pltpu.make_async_remote_copy(
                bsend.at[q, partner], brecv.at[q, ctx], bs_sem.at[q, i], br_sem.at[q, i],
                device_id=(partner, ch), device_id_type=MESH)
            copy.start()
            copies.append(copy)
        brecv[q, ctx] = bsend[q, ctx]
        returned.append(copies)
    loads[6].wait()
    loads[7].wait()
    w_load.wait()
    def gate(q):
        mask = low_half[:SPAN]
        for t in range(8):
            columns = slice(t * LANES, (t + 1) * LANES)
            even, odd = brecv[q, 2 * t].astype(jnp.float32), brecv[q, 2 * t + 1].astype(jnp.float32)
            for part in range(2):
                rows = slice(part * HALF + q * SPAN, part * HALF + (q + 1) * SPAN)
                if part == 0:
                    convolved = jnp.where(mask, even, pltpu.roll(odd, HALF, 1))
                else:
                    convolved = jnp.where(mask, pltpu.roll(even, HALF, 1), odd)
                values = v[rows, columns].astype(jnp.float32)
                gates = g[rows, columns].astype(jnp.float32)
                total = ((convolved + bias_ref[0:1, columns] * values) * gates).astype(jnp.bfloat16)
                gated[q * HALF + part * SPAN:q * HALF + (part + 1) * SPAN, columns] = total

    def project(distance, part, to_core, rows=slice(0, ROWS)):
        start = (shifted(z, distance) * 2 + to_core) * 1024 + part * 512
        return dot(gated[rows, :], w[:, pl.ds(pl.multiple_of(start, 512), 512)])

    first_rows, last_rows = slice(0, HALF), slice(HALF, ROWS)
    everything = slice(0, ROWS)

    def to_other(distance, part, rows=everything):
        i = 2 * distance + part
        psend[i, rows, :] = project(distance, part, 1 - core, rows).astype(jnp.bfloat16)
        copy = pltpu.make_async_remote_copy(
            psend.at[i, rows], precv.at[i, rows], ps_sem.at[i], pr_sem.at[i], device_id=other, device_id_type=MESH)
        copy.start()
        pair[distance, part] = copy

    def with_other(distance, part, own, rows=everything):
        pair[distance, part].wait_recv()
        return own + precv[2 * distance + part, rows, :].astype(jnp.float32)

    def ring(i, device, rows=everything):
        copy = pltpu.make_async_remote_copy(
            ring_s.at[i, rows], ring_r.at[i, rows], rs_sem.at[i], rr_sem.at[i], device_id=device, device_id_type=MESH)
        copy.start()
        rings[i] = copy

    pair = {}
    rings = {}

    for copy in returned[0]:
        copy.wait_recv()
    gate(0)
    for i, distance, part, to_core, device in (
            (6, 1, 1, core, up), (7, 3, 0, core, down), (8, 1, 1, 1 - core, up_crossed), (9, 3, 0, 1 - core, down_crossed)):
        ring_s[i, first_rows, :] = project(distance, part, to_core, first_rows).astype(jnp.bfloat16)
        ring(i, device, first_rows)
    for copy in returned[1]:
        copy.wait_recv()
    gate(1)
    for distance, part in ((2, 0), (2, 1)):
        to_other(distance, part)
    for distance, part in ((1, 1), (3, 0)):
        to_other(distance, part, last_rows)
    for part in range(2):
        keep[part] = project(2, part, core)
    for part, device in ((0, up), (1, down)):
        ring_s[part] = with_other(2, part, keep[part]).astype(jnp.bfloat16)
        ring(part, device)
    for distance, part in ((1, 0), (3, 1)):
        to_other(distance, part)
    for i, distance, part in ((0, 1, 1), (1, 3, 0)):
        keep[i, last_rows, :] = project(distance, part, core, last_rows)
    for i, distance, part, device in ((2, 1, 1, up), (3, 3, 0, down)):
        ring_s[i, last_rows, :] = with_other(distance, part, keep[i - 2, last_rows, :], last_rows).astype(jnp.bfloat16)
        ring(i, device, last_rows)
    relay[0], relay[1] = project(1, 0, core), project(3, 1, core)
    for i, distance, part in ((0, 1, 0), (1, 3, 1)):
        relay[i] = with_other(distance, part, relay[i])
    for i, device in ((4, up), (5, down)):
        rings[i - 4].wait_recv()
        ring_s[i] = (relay[i - 4] + ring_r[i - 4].astype(jnp.float32)).astype(jnp.bfloat16)
        ring(i, device)
    for part in range(2):
        to_other(0, part)
    for part in range(2):
        keep[part] = project(0, part, core)
    for part in range(2):
        keep[part] = with_other(0, part, keep[part])
    for part, slots in ((0, (7, 9, 3)), (1, (6, 8, 2))):
        for i in slots:
            rows = last_rows if i < 4 else first_rows
            rings[i].wait_recv()
            keep[part, rows, :] += ring_r[i, rows, :].astype(jnp.float32)
    for part, i in ((0, 4), (1, 5)):
        rings[i].wait_recv()
        total = keep[part] + ring_r[i].astype(jnp.float32)
        for q in range(2):
            for half in range(2):
                token, row = half * HALF + q * SPAN, q * HALF + half * SPAN
                out_ref[token:token + SPAN, part * 512:(part + 1) * 512] = total[row:row + SPAN]
    for copies in (*returned, pair.values(), rings.values()):
        for copy in copies:
            copy.wait_send()


def on_device(keyed_values, gate_values, long_filter, skip_bias, out_weight):
    first, middle, middle_back, last = (jnp.asarray(t) for t in tables())
    bf, f32 = jnp.bfloat16, jnp.float32
    hbm = pl.BlockSpec(memory_space=pltpu.HBM)
    vmem = pl.BlockSpec(memory_space=pltpu.VMEM)
    dma = pltpu.SemaphoreType.DMA
    hops = len(ROUTES)
    return pl.pallas_call(
        kernel,
        out_shape=pltpu.VMEM((ROWS, 1024), f32),
        in_specs=[hbm, hbm, hbm, hbm, hbm, hbm, hbm, hbm, hbm],
        out_specs=vmem,
        scratch_shapes=[
            pltpu.VMEM((ROWS, 1024), bf),
            pltpu.VMEM((ROWS, 1024), bf),
            pltpu.VMEM((ROWS, 1024), f32),
            pltpu.VMEM((1, 1024), f32),
            pltpu.VMEM((1024, 8192), bf),
            pltpu.VMEM((512, 256), bf),
            pltpu.VMEM((16, 256, 256), bf),
            pltpu.VMEM((16, 256, 256), bf),
            pltpu.VMEM((256, 512), bf),
            pltpu.VMEM((BLOCKS, ROWS, LANES), bf),
            pltpu.VMEM((BLOCKS, ROWS, LANES), bf),
            pltpu.VMEM((16, 2, ROWS, LANES), bf),
            pltpu.VMEM((16, 2, HALF, LANES), bf),
            pltpu.VMEM((2, BLOCKS, SPAN, LANES), bf),
            pltpu.VMEM((2, BLOCKS, SPAN, LANES), bf),
            pltpu.VMEM((ROWS, 1024), bf),
            pltpu.VMEM((8, ROWS, 512), bf),
            pltpu.VMEM((8, ROWS, 512), bf),
            pltpu.VMEM((10, ROWS, 512), bf),
            pltpu.VMEM((10, ROWS, 512), bf),
            pltpu.VMEM((2, ROWS, 512), f32),
            pltpu.VMEM((2, ROWS, 512), f32),
            dma((8,)),
            dma,
            dma((hops,)),
            dma((hops,)),
            dma((2, hops)),
            dma((2, hops)),
            dma((8,)),
            dma((8,)),
            dma((10,)),
            dma((10,)),
        ],
        compiler_params=pltpu.CompilerParams(
            collective_id=0, has_side_effects=True, vmem_limit_bytes=60 << 20),
        cost_estimate=pl.CostEstimate(flops=3 << 30, bytes_accessed=24 << 20, transcendentals=0),
    )(keyed_values, gate_values, long_filter, skip_bias.reshape(1, 1024), out_weight, first, middle, middle_back, last)


def solution(mesh):
    return jax.shard_map(
        on_device,
        mesh=mesh,
        in_specs=(P("ctx", "ch"), P("ctx", "ch"), P("ctx", "ch"), P("ch"), P("ch", None)),
        out_specs=P("ctx", "ch"),
        check_vma=False,
    )
```
